32 devices in a mesh: layer: 8 (over y, x, core), row: 4 (over z).
Axes of the slice: x: 2, y: 2, z: 4, core: 2. Of those that a mesh axis runs over, the one named last changes fastest.
Arguments:
- operator: bfloat16 [2, 8, 4096, 4096], P(None, 'layer', 'row'), may hold values from -0.0625 to 0.0625
- sources: bfloat16 [2, 8, 4096, 512], P(None, 'layer', 'row'), may hold values from -3 to 3
- boundary: bfloat16 [2, 4096, 512], P(None, 'row'), may hold values from -6 to 6
Outputs:
- traces: float32 [2, 8, 4096, 512], P(None, 'layer', 'row')
The draws below stay inside these ranges and needn't reach their ends.
All inputs are finite; a program needn't handle non-finite values.
Results may differ from the reference program's by a relative error of at most 0.015.
Values may be sent and summed in bfloat16 or wider, within the bound.
A program may use at most 128 MiB of HBM per device.

```python
import jax
import jax.numpy as jnp

M = 4096
SRC = 512
LAYERS = 8


def level_of(own_key, shape, pieces, low, high):
    level, own = 1.0, jax.random.fold_in(own_key, 6)
    for dim, blocks in pieces:
        draws = jnp.exp(jax.random.uniform(jax.random.fold_in(own, dim), (blocks,), jnp.float32, low / len(pieces), high / len(pieces)))
        level = level * jnp.repeat(draws, shape[dim] // blocks).reshape([-1 if axis == dim else 1 for axis in range(len(shape))])
    return level


def centred(key, extent, spread, limit, shards=(), held_as=jnp.bfloat16):
    array = spread * jax.random.normal(key, extent, jnp.float32)
    if shards:
        array = array * level_of(key, extent, shards, -0.22, 0.18)
    return jnp.clip(array, -limit, limit).astype(held_as)


def setup_inputs(seed: int = 0) -> dict:
    seeds = jax.random.split(jax.random.key(seed), 4)
    operator = centred(seeds[0], (2, LAYERS, M, M), (2 * M) ** -0.5, 0.0625, ((1, 8), (2, 4)))
    sources = centred(seeds[1], (2, LAYERS, M, SRC), 0.5, 3.0, ((1, 8), (2, 4)))
    boundary = centred(seeds[2], (2, M, SRC), 1.0, 6.0, ((1, 4),))
    return dict(operator=operator, sources=sources, boundary=boundary)


def reference(operator, sources, boundary):
    incoming = boundary
    outputs = []
    for level in range(LAYERS):
        real = operator[0, level]
        imag = operator[1, level]
        part_re = jnp.dot(real, incoming[0], preferred_element_type=jnp.float32) - jnp.dot(imag, incoming[1], preferred_element_type=jnp.float32)
        part_im = jnp.dot(real, incoming[1], preferred_element_type=jnp.float32) + jnp.dot(imag, incoming[0], preferred_element_type=jnp.float32)
        result = jnp.stack([part_re, part_im], axis=0) + sources[:, level].astype(jnp.float32)
        outputs.append(result)
        incoming = result.astype(jnp.bfloat16)
    return jnp.stack(outputs, axis=1)
```

```python
import functools

import jax
import jax.numpy as jnp
from jax import lax
from jax.experimental import pallas as pl
from jax.experimental.pallas import tpu as pltpu
from jax.sharding import PartitionSpec as P

MESH = pl.DeviceIdType.MESH
WIDTH = 32
TILE = 256


def contract(left, weights):
    return lax.dot_general(
        left, weights, (((1,), (1,)), ((), ())), preferred_element_type=jnp.float32
    )


def sweep(
    depth,
    rows,
    operator_ref,
    source_ref,
    entering_ref,
    trace_ref,
    weights,
    incoming,
    outgoing,
    load_sem,
    arrived,
    sent_up,
    sent_down,
    sent_on,
):
    level, me = lax.axis_index("layer"), lax.axis_index("row")
    count, double, local = source_ref.shape
    width = double // 2
    has_up, has_down = me < rows - 1, me > 0
    has_next, has_prev = level < depth - 1, level > 0

    def load(part):
        return pltpu.make_async_copy(
            operator_ref.at[:, 0, :, pl.ds(pl.multiple_of(part * local, local), local)],
            weights.at[part],
            load_sem.at[part],
        )

    def enter(batch):
        return pltpu.make_async_copy(
            entering_ref.at[batch], incoming.at[batch, me], arrived.at[batch, me]
        )

    def along(batch, part, by, sem):
        return pltpu.make_async_remote_copy(
            src_ref=incoming.at[batch, part],
            dst_ref=incoming.at[batch, part],
            send_sem=sem.at[lax.rem(batch, 2), part],
            recv_sem=arrived.at[batch, part],
            device_id={"row": me + by},
            device_id_type=MESH,
        )

    def onward(batch):
        return pltpu.make_async_remote_copy(
            src_ref=outgoing.at[batch],
            dst_ref=incoming.at[batch, me],
            send_sem=sent_on.at[lax.rem(batch, 2)],
            recv_sem=arrived.at[batch, me],
            device_id={"layer": level + 1},
            device_id_type=MESH,
        )

    for part in range(rows):
        load(lax.rem(me + part, rows)).start()

    @pl.when(level == 0)
    def _():
        @pl.loop(0, count)
        def _(batch):
            enter(batch).start()

    barrier = pltpu.get_barrier_semaphore()
    for there, where in (
        (has_up, {"row": me + 1}),
        (has_down, {"row": me - 1}),
        (has_next, {"layer": level + 1}),
        (has_prev, {"layer": level - 1}),
    ):
        @pl.when(there)
        def _(where=where):
            pl.semaphore_signal(barrier, inc=1, device_id=where, device_id_type=MESH)

    pl.semaphore_wait(
        barrier, sum(x.astype(jnp.int32) for x in (has_up, has_down, has_next, has_prev))
    )

    def multiply(batch, part):
        @pl.when(batch == 0)
        def _():
            load(part).wait()

        x = incoming[batch, part]
        for at in range(0, local, TILE):
            cols = slice(at, at + TILE)
            by_re = contract(x, weights[part, 0, cols, :])
            by_im = contract(x, weights[part, 1, cols, :])
            trace_ref[batch, :width, cols] += by_re[:width] - by_im[width:]
            trace_ref[batch, width:, cols] += by_re[width:] + by_im[:width]

    def receive(batch, part):
        pltpu.make_async_copy(
            incoming.at[batch, part], incoming.at[batch, part], arrived.at[batch, part]
        ).wait()

    def drain(batch):
        @pl.loop(0, rows)
        def _(part):
            @pl.when(jnp.logical_and(has_up, part <= me))
            def _():
                along(batch, part, 1, sent_up).wait_send()

            @pl.when(jnp.logical_and(has_down, part >= me))
            def _():
                along(batch, part, -1, sent_down).wait_send()

        @pl.when(has_next)
        def _():
            onward(batch).wait_send()

    @pl.loop(0, count)
    def _(batch):
        trace_ref[batch] = source_ref[batch].astype(jnp.float32)

        @pl.when(batch >= 2)
        def _():
            drain(batch - 2)

        @pl.loop(0, rows)
        def _(hop):
            below, above = me - hop, me + hop
            from_below = below >= 0
            from_above = jnp.logical_and(hop > 0, above < rows)

            @pl.when(from_below)
            def _():
                receive(batch, below)

                @pl.when(has_up)
                def _():
                    along(batch, below, 1, sent_up).start()

            @pl.when(jnp.logical_and(hop == 0, has_down))
            def _():
                along(batch, me, -1, sent_down).start()

            @pl.when(from_above)
            def _():
                receive(batch, above)

                @pl.when(has_down)
                def _():
                    along(batch, above, -1, sent_down).start()

            @pl.when(from_below)
            def _():
                multiply(batch, below)

            @pl.when(from_above)
            def _():
                multiply(batch, above)

        @pl.when(has_next)
        def _():
            outgoing[batch] = trace_ref[batch].astype(jnp.bfloat16)
            onward(batch).start()

    for batch in range(max(count - 2, 0), count):
        drain(batch)


def on_device(depth, rows, operator, sources, boundary):
    local, total = sources.shape[2], sources.shape[3]
    width = WIDTH
    count = total // width

    def batches(value):
        value = jnp.swapaxes(value, 1, 2).reshape(2, count, width, local)
        return jnp.swapaxes(value, 0, 1).reshape(count, 2 * width, local)

    flops = 2 * 4 * local * operator.shape[3] * total
    traces = pl.pallas_call(
        functools.partial(sweep, depth, rows),
        out_shape=jax.ShapeDtypeStruct((count, 2 * width, local), jnp.float32),
        in_specs=[
            pl.BlockSpec(memory_space=pl.ANY),
            pl.BlockSpec(memory_space=pltpu.VMEM),
            pl.BlockSpec(memory_space=pl.ANY),
        ],
        out_specs=pl.BlockSpec(memory_space=pltpu.VMEM),
        scratch_shapes=[
            pltpu.VMEM((rows, 2, local, local), jnp.bfloat16),
            pltpu.VMEM((count, rows, 2 * width, local), jnp.bfloat16),
            pltpu.VMEM((count, 2 * width, local), jnp.bfloat16),
            pltpu.SemaphoreType.DMA((rows,)),
            pltpu.SemaphoreType.DMA((count, rows)),
            pltpu.SemaphoreType.DMA((2, rows)),
            pltpu.SemaphoreType.DMA((2, rows)),
            pltpu.SemaphoreType.DMA((2,)),
        ],
        compiler_params=pltpu.CompilerParams(
            collective_id=0, has_side_effects=True, vmem_limit_bytes=50 << 20
        ),
        cost_estimate=pl.CostEstimate(
            flops=flops, bytes_accessed=2 * operator.size, transcendentals=0
        ),
    )(operator, batches(sources[:, 0]), batches(boundary))
    traces = traces.reshape(count, 2, width, local)
    return traces.transpose(1, 3, 0, 2).reshape(2, 1, local, total)


def solution(mesh):
    placed = (P(None, "layer", "row", None), P(None, "layer", "row", None), P(None, "row", None))
    return jax.shard_map(
        functools.partial(on_device, mesh.shape["layer"], mesh.shape["row"]),
        mesh=mesh,
        in_specs=placed,
        out_specs=P(None, "layer", "row", None),
        check_vma=False,
    )
```

```python
import functools

import jax
import jax.numpy as jnp
from jax import lax
from jax.experimental import pallas as pl
from jax.experimental.pallas import tpu as pltpu
from jax.sharding import PartitionSpec as P

MESH = pl.DeviceIdType.MESH
WIDTH = 32
TILE = 256
REACH = 2
NEAR = (2, -2, 1, -1)
SLOTS = 4


def contract(left, weights):
    return lax.dot_general(
        left, weights, (((1,), (1,)), ((), ())), preferred_element_type=jnp.float32
    )


def sweep(
    depth,
    rows,
    operator_ref,
    source_ref,
    entering_ref,
    trace_ref,
    weights,
    incoming,
    outgoing,
    load_sem,
    arrived,
    sent_first,
    sent_on,
    passed,
):
    level, me = lax.axis_index("layer"), lax.axis_index("row")
    count, _, _, width, local = incoming.shape
    has_next, has_prev = level < depth - 1, level > 0
    first, last = level == 0, level == depth - 1
    others = [side * by for by in range(1, rows) for side in (1, -1)]

    def inside(row):
        return jnp.logical_and(row >= 0, row < rows)

    def both(*flags):
        return functools.reduce(jnp.logical_and, flags)

    def columns(batch):
        return pl.ds(pl.multiple_of(batch * width, width), width)

    def load(part):
        return pltpu.make_async_copy(
            operator_ref.at[:, 0, :, pl.ds(pl.multiple_of(part * local, local), local)],
            weights.at[part],
            load_sem.at[part],
        )

    def enter(batch):
        return pltpu.make_async_copy(
            entering_ref.at[:, columns(batch)], incoming.at[batch, me], arrived.at[batch, me]
        )

    def send_first(batch, by):
        return pltpu.make_async_remote_copy(
            src_ref=entering_ref.at[:, columns(batch)],
            dst_ref=incoming.at[batch, me],
            send_sem=sent_first.at[lax.rem(batch, SLOTS), by + rows - 1],
            recv_sem=arrived.at[batch, me],
            device_id={"layer": lax.rem(level + 1, depth), "row": me + by},
            device_id_type=MESH,
        )

    def send_on(batch, by):
        return pltpu.make_async_remote_copy(
            src_ref=outgoing.at[batch],
            dst_ref=incoming.at[batch, me],
            send_sem=sent_on.at[lax.rem(batch, 2), by + REACH],
            recv_sem=arrived.at[batch, me],
            device_id={"layer": level + 1, "row": me + by},
            device_id_type=MESH,
        )

    def forward(batch, part, by):
        return pltpu.make_async_remote_copy(
            src_ref=incoming.at[batch, part],
            dst_ref=incoming.at[batch, part],
            send_sem=passed.at[lax.rem(batch, 2), part],
            recv_sem=arrived.at[batch, part],
            device_id={"row": me + by},
            device_id_type=MESH,
        )

    @pl.when(first)
    def _():
        @pl.loop(0, count)
        def _(batch):
            enter(batch).start()

    for part in range(rows):
        load(lax.rem(me + part, rows)).start()

    barrier = pltpu.get_barrier_semaphore()
    peers = [(inside(me + by), {"row": me + by}) for by in (1, -1)]
    for by in others:
        peers.append((both(first, inside(me + by)), {"layer": lax.rem(level + depth - 1, depth), "row": me + by}))
        peers.append((both(last, inside(me + by)), {"layer": lax.rem(level + 1, depth), "row": me + by}))
    for by in (*NEAR, 0):
        peers.append((both(has_next, inside(me + by)), {"layer": level + 1, "row": me + by}))
        peers.append((both(has_prev, inside(me + by)), {"layer": level - 1, "row": me + by}))
    for there, where in peers:
        @pl.when(there)
        def _(where=where):
            pl.semaphore_signal(barrier, inc=1, device_id=where, device_id_type=MESH)
    pl.semaphore_wait(barrier, sum(there.astype(jnp.int32) for there, _ in peers))

    def settle(batch):
        for by in others:
            @pl.when(inside(me + by))
            def _(by=by):
                send_first(batch, by).wait_send()

    @pl.when(last)
    def _():
        @pl.loop(0, count)
        def _(batch):
            @pl.when(batch >= SLOTS)
            def _():
                settle(batch - SLOTS)

            for by in others:
                @pl.when(inside(me + by))
                def _(by=by):
                    send_first(batch, by).start()

        @pl.loop(max(count - SLOTS, 0), count)
        def _(batch):
            settle(batch)

    def multiply(batch, part):
        @pl.when(batch == 0)
        def _():
            load(part).wait()

        x = incoming[batch, part].reshape(2 * width, local)
        for at in range(0, local, TILE):
            cols = slice(at, at + TILE)
            by_re = contract(x, weights[part, 0, cols, :])
            by_im = contract(x, weights[part, 1, cols, :])
            trace_ref[0, columns(batch), cols] += by_re[:width] - by_im[width:]
            trace_ref[1, columns(batch), cols] += by_re[width:] + by_im[:width]

    def receive(batch, part):
        pltpu.make_async_copy(
            incoming.at[batch, part], incoming.at[batch, part], arrived.at[batch, part]
        ).wait()

    def drain(batch):
        for by in (*NEAR, 0):
            @pl.when(both(has_next, inside(me + by)))
            def _(by=by):
                send_on(batch, by).wait_send()

        @pl.loop(0, rows)
        def _(part):
            @pl.when(both(has_prev, me - part >= REACH, me < rows - 1))
            def _():
                forward(batch, part, 1).wait_send()

            @pl.when(both(has_prev, part - me >= REACH, me > 0))
            def _():
                forward(batch, part, -1).wait_send()

    def take(batch, distance, side):
        part = me - side * distance
        @pl.when(inside(part))
        def _():
            receive(batch, part)

            @pl.when(both(has_prev, distance >= REACH, inside(me + side)))
            def _():
                forward(batch, part, side).start()

    @pl.loop(0, count)
    def _(batch):
        trace_ref[:, columns(batch)] = source_ref[:, columns(batch)].astype(jnp.float32)

        @pl.when(batch >= 2)
        def _():
            drain(batch - 2)

        @pl.loop(0, rows)
        def _(distance):
            @pl.when(distance == 1)
            def _():
                take(batch, REACH, 1)
                take(batch, REACH, -1)

            for side in (1, -1):
                part = me - side * distance

                @pl.when(jnp.logical_and(distance != REACH, distance > 0 if side < 0 else distance >= 0))
                def _(side=side):
                    take(batch, distance, side)

                @pl.when(jnp.logical_and(inside(part), distance > 0 if side < 0 else distance >= 0))
                def _(part=part):
                    multiply(batch, part)

        @pl.when(has_next)
        def _():
            outgoing[batch] = trace_ref[:, columns(batch)].astype(jnp.bfloat16)
            for by in (*NEAR, 0):
                @pl.when(inside(me + by))
                def _(by=by):
                    send_on(batch, by).start()

    for batch in range(max(count - 2, 0), count):
        drain(batch)


def on_device(depth, rows, operator, sources, boundary):
    local, total = sources.shape[2], sources.shape[3]
    width = WIDTH
    count = total // width

    flops = 2 * 4 * local * operator.shape[3] * total
    traces = pl.pallas_call(
        functools.partial(sweep, depth, rows),
        out_shape=jax.ShapeDtypeStruct((2, total, local), jnp.float32),
        in_specs=[
            pl.BlockSpec(memory_space=pl.ANY),
            pl.BlockSpec(memory_space=pltpu.VMEM),
            pl.BlockSpec(memory_space=pl.ANY),
        ],
        out_specs=pl.BlockSpec(memory_space=pltpu.VMEM),
        scratch_shapes=[
            pltpu.VMEM((rows, 2, local, local), jnp.bfloat16),
            pltpu.VMEM((count, rows, 2, width, local), jnp.bfloat16),
            pltpu.VMEM((count, 2, width, local), jnp.bfloat16),
            pltpu.SemaphoreType.DMA((rows,)),
            pltpu.SemaphoreType.DMA((count, rows)),
            pltpu.SemaphoreType.DMA((SLOTS, 2 * rows - 1)),
            pltpu.SemaphoreType.DMA((2, 2 * REACH + 1)),
            pltpu.SemaphoreType.DMA((2, rows)),
        ],
        compiler_params=pltpu.CompilerParams(
            collective_id=0, has_side_effects=True, vmem_limit_bytes=50 << 20
        ),
        cost_estimate=pl.CostEstimate(
            flops=flops, bytes_accessed=2 * operator.size, transcendentals=0
        ),
    )(operator, jnp.swapaxes(sources[:, 0], 1, 2), jnp.swapaxes(boundary, 1, 2))
    return jnp.swapaxes(traces, 1, 2)[:, None]


def solution(mesh):
    placed = (P(None, "layer", "row", None), P(None, "layer", "row", None), P(None, "row", None))
    return jax.shard_map(
        functools.partial(on_device, mesh.shape["layer"], mesh.shape["row"]),
        mesh=mesh,
        in_specs=placed,
        out_specs=P(None, "layer", "row", None),
        check_vma=False,
    )
```
